32 devices in a mesh: genome: 8 (over y, x, core), sample: 4 (over z).
Axes of the slice: x: 2, y: 2, z: 4, core: 2. Of those that a mesh axis runs over, the one named last changes fastest.
Arguments:
- genotypes: bfloat16 [32768, 4096], P('sample', 'genome'), may hold values from 0 to 2
- probes: bfloat16 [32768, 1024], P('sample', 'genome'), may hold values from -12 to 12
- covariates: float32 [20, 32768], P(None, 'sample')
- probe_locus: int32 [1024], replicated, may hold values from 0 to 39999, as said below
- probe_counts: int32 [8], replicated, may hold values from 32 to 128, as said below
- reach: int32 [8], P('genome'), may hold values from 1 to 2, as said below
- positions: int32 [4096], P(('genome', 'sample')), may hold values from 0 to 39999, as said below
Outputs:
- zscores: float32 [4096, 640], P(('genome', 'sample'))
The draws below stay inside these ranges and needn't reach their ends.
Inputs may be any that keep to these rules, and one draw needn't show every extreme that they name: `probe_locus`: slot q of block b has a position in b * 5000 to (b + 1) * 5000 - 1. `probe_counts`: some block holds exactly 128. `reach`: some block reaches exactly 2. `positions`: variants of block b lie in b * 5000 to (b + 1) * 5000 - 1.
All inputs are finite; a program needn't handle non-finite values.
Results may differ from the reference program's by a relative error of at most 0.0041.
Values may be sent and summed in bfloat16 or wider, within the bound.
A program may use at most 128 MiB of HBM per device.

```python
import math
import jax
import jax.numpy as jnp
from jax import lax

K = 20
VB = 512
PB = 128
REACH = 2
SPAN = 5000
WIN = 10000
NBLK = 8
SAMPLES = 32768
VARIANTS = 4096
PROBES = 1024


def covariate_rows(key):
    return jax.random.normal(key, (K, SAMPLES), jnp.float32)


def depth_rows(key, low, high):
    ramp = jnp.arange(SAMPLES, dtype=jnp.float32) / SAMPLES
    jitter = jax.random.uniform(key, (SAMPLES,), jnp.float32, 0.7, 1.0)
    return ((low + (high - low) * ramp) * jitter)[:, None]


def draw_covariates(key, part):
    return covariate_rows(key)


def draw_genotypes(key, part):
    covar = covariate_rows(key)
    key = jax.random.fold_in(key, 11)
    keys = jax.random.split(key, 4)
    freq = jnp.exp(jax.random.uniform(keys[0], (1, VARIANTS), jnp.float32, math.log(0.05), 0.0))
    depth = depth_rows(keys[1], 0.3, 1.0)
    loads = jax.random.normal(keys[2], (3, VARIANTS), jnp.float32) * 0.8
    effect = covar[0][:, None] * loads[0][None, :] + covar[1][:, None] * loads[1][None, :]
    effect = effect + covar[2][:, None] * loads[2][None, :]
    noise = jax.random.normal(keys[3], (SAMPLES, VARIANTS), jnp.float32)
    return (freq * depth * (1.0 + jnp.tanh(effect + noise))).astype(jnp.bfloat16)


def draw_probes(key, part):
    covar = covariate_rows(key)
    key = jax.random.fold_in(key, 12)
    keys = jax.random.split(key, 4)
    spread = jnp.exp(jax.random.uniform(keys[0], (1, PROBES), jnp.float32, math.log(0.3), math.log(3.0)))
    depth = depth_rows(keys[1], 0.5, 2.0)
    loads = jax.random.normal(keys[2], (4, PROBES), jnp.float32)
    effect = covar[0][:, None] * loads[0][None, :] + covar[1][:, None] * loads[1][None, :]
    effect = effect + covar[3][:, None] * loads[2][None, :] + covar[4][:, None] * loads[3][None, :]
    noise = jax.random.normal(keys[3], (SAMPLES, PROBES), jnp.float32)
    return jnp.clip(spread * (effect + depth * noise), -12.0, 12.0).astype(jnp.bfloat16)


def block_positions(key, per_block):
    owner = jnp.arange(NBLK * per_block, dtype=jnp.int32) // per_block
    return jax.random.randint(key, (NBLK * per_block,), 0, SPAN, jnp.int32) + owner * SPAN


def draw_probe_locus(key, part):
    key = jax.random.fold_in(key, 21)
    return block_positions(key, PB)


def draw_positions(key, part):
    key = jax.random.fold_in(key, 22)
    return block_positions(key, VB)


def draw_probe_counts(key, part):
    key = jax.random.fold_in(key, 23)
    first, second = jax.random.split(key)
    base = jax.random.randint(first, (NBLK,), PB // 4, PB + 1, jnp.int32)
    fullest = jax.random.randint(second, (), 0, NBLK, jnp.int32)
    return jnp.where(jnp.arange(NBLK, dtype=jnp.int32) == fullest, PB, base).astype(jnp.int32)


def draw_reach(key, part):
    key = jax.random.fold_in(key, 24)
    first, second = jax.random.split(key)
    base = jax.random.randint(first, (NBLK,), 1, REACH + 1, jnp.int32)
    widest = jax.random.randint(second, (), 0, NBLK, jnp.int32)
    return jnp.where(jnp.arange(NBLK, dtype=jnp.int32) == widest, REACH, base).astype(jnp.int32)


def setup_inputs(seed: int = 0) -> dict:
    arg_keys = jax.random.split(jax.random.key(seed), 8)
    return {
        "genotypes": draw_genotypes(jax.random.fold_in(arg_keys[7], 71), 0),
        "probes": draw_probes(jax.random.fold_in(arg_keys[7], 71), 0),
        "covariates": draw_covariates(jax.random.fold_in(arg_keys[7], 71), 0),
        "probe_locus": draw_probe_locus(jax.random.fold_in(arg_keys[7], 71), 0),
        "probe_counts": draw_probe_counts(jax.random.fold_in(arg_keys[7], 71), 0),
        "reach": draw_reach(jax.random.fold_in(arg_keys[7], 71), 0),
        "positions": draw_positions(jax.random.fold_in(arg_keys[7], 71), 0),
    }


def residualize(data, basis, factor):
    cross = jnp.dot(basis, data.astype(jnp.float32), precision=lax.Precision.HIGHEST)
    coef = jax.scipy.linalg.cho_solve((factor, True), cross)
    fitted = jnp.dot(basis.T, coef, precision=lax.Precision.HIGHEST)
    return (data.astype(jnp.float32) - fitted).astype(jnp.bfloat16)

def reference(genotypes, probes, covariates, probe_locus, probe_counts, reach, positions):
    samples = genotypes.shape[0]
    nblk = probe_counts.shape[0]
    width_v = genotypes.shape[1] // nblk
    width_p = probe_locus.shape[0] // nblk
    wide = (2 * REACH + 1) * width_p
    ncov = covariates.shape[0]
    basis = jnp.concatenate([jnp.ones((1, samples), jnp.float32), covariates], 0)
    gram = jnp.dot(basis, basis.T, precision=lax.Precision.HIGHEST)
    factor = jnp.linalg.cholesky(gram)
    probe_res = residualize(probes, basis, factor)
    padded_probe = jnp.pad(probe_res, ((0, 0), (REACH * width_p, REACH * width_p)))
    padded_start = jnp.pad(probe_locus, (REACH * width_p, REACH * width_p))
    padded_count = jnp.pad(probe_counts, (REACH, REACH))
    column = jnp.arange(wide, dtype=jnp.int32)
    offset = column // width_p - REACH
    slot = column % width_p
    scale = jnp.sqrt(jnp.float32(samples - ncov - 2))

    def one_block(block):
        block = block.astype(jnp.int32)
        geno = lax.dynamic_slice_in_dim(genotypes, block * width_v, width_v, 1)
        geno_res = residualize(geno, basis, factor)
        window = lax.dynamic_slice_in_dim(padded_probe, block * width_p, wide, 1)
        gres32 = geno_res.astype(jnp.float32)
        win32 = window.astype(jnp.float32)
        gnorm = lax.optimization_barrier(jnp.sum(gres32 * gres32, 0))
        pnorm = lax.optimization_barrier(jnp.sum(win32 * win32, 0))
        num = jnp.dot(gres32.T, win32)
        starts = lax.dynamic_slice_in_dim(padded_start, block * width_p, wide, 0)
        counted = lax.dynamic_slice_in_dim(padded_count, block, 2 * REACH + 1, 0)[column // width_p]
        where_v = lax.dynamic_slice_in_dim(positions, block * width_v, width_v, 0)
        inside = (block + offset >= 0) & (block + offset < nblk)
        tested = inside & (slot < counted) & (jnp.abs(offset) <= reach[block])
        tested = tested[None, :] & (jnp.abs(where_v[:, None] - starts[None, :]) <= WIN)
        value = scale * num / (jnp.sqrt(gnorm + 1e-06)[:, None] * jnp.sqrt(pnorm + 1e-06)[None, :])
        return jnp.where(tested, value, jnp.float32(0.0))
    blocks = lax.map(one_block, jnp.arange(nblk, dtype=jnp.int32))
    return blocks.reshape(nblk * width_v, wide)
```

```python
import functools

import jax
import jax.numpy as jnp
from jax import lax
from jax.experimental import pallas as pl
from jax.experimental.pallas import tpu as pltpu
from jax.sharding import PartitionSpec as P

REACH = 2
WIN = 10000


def from_behind(value, axis, steps):
    count = lax.axis_size(axis)
    first, last = (max(0, -steps), min(count, count - steps))
    return lax.ppermute(value, axis, [(source, source + steps) for source in range(first, last)])


def fitted_part(data, basis, coef_sum, factor):
    coef = jax.scipy.linalg.cho_solve((factor, True), coef_sum)
    fitted = jnp.dot(basis.T, coef, precision=lax.Precision.HIGHEST)
    return (data.astype(jnp.float32) - fitted).astype(jnp.bfloat16)


def variant_products(left, right):
    return lax.dot_general(
        left, right, (((0,), (0,)), ((), ())), preferred_element_type=jnp.float32
    )


def local(genotypes, probes, covariates, probe_locus, probe_counts, reach, positions):
    rows = genotypes.shape[0]
    width_v = genotypes.shape[1]
    width_p = probes.shape[1]
    ncov = covariates.shape[0]
    nblk = probe_counts.shape[0]
    wide = (2 * REACH + 1) * width_p
    basis = jnp.concatenate([jnp.ones((1, rows), jnp.float32), covariates], 0)
    gram = jnp.dot(basis, basis.T, precision=lax.Precision.HIGHEST)
    cross_geno = jnp.dot(basis, genotypes.astype(jnp.float32), precision=lax.Precision.HIGHEST)
    cross_probe = jnp.dot(basis, probes.astype(jnp.float32), precision=lax.Precision.HIGHEST)
    gram, cross_geno, cross_probe = lax.psum((gram, cross_geno, cross_probe), "sample")
    factor = jnp.linalg.cholesky(gram)
    geno_res = fitted_part(genotypes, basis, cross_geno, factor)
    probe_res = fitted_part(probes, basis, cross_probe, factor)
    pieces = {0: probe_res}
    for direction in (1, -1):
        current = probe_res
        for stepper in range(1, REACH + 1):
            current = from_behind(current, "genome", -direction)
            pieces[direction * stepper] = current
    window = jnp.concatenate([pieces[offset] for offset in range(-REACH, REACH + 1)], 1)
    gres32 = geno_res.astype(jnp.float32)
    win32 = window.astype(jnp.float32)
    gnorm, pnorm = lax.psum((jnp.sum(gres32 * gres32, 0), jnp.sum(win32 * win32, 0)), "sample")
    share = width_v // lax.axis_size("sample")
    first_row = lax.axis_index("sample") * share
    total = lax.psum(variant_products(geno_res, window), "sample")
    mine = lax.dynamic_slice_in_dim(total, first_row, share, 0)
    gnorm_mine = lax.dynamic_slice_in_dim(gnorm, first_row, share, 0)
    block = lax.axis_index("genome")
    column = jnp.arange(wide, dtype=jnp.int32)
    offset_of = column // width_p - REACH
    slot_of = column % width_p
    padded_start = jnp.pad(probe_locus, (REACH * width_p, REACH * width_p))
    padded_count = jnp.pad(probe_counts, (REACH, REACH))
    starts = lax.dynamic_slice_in_dim(padded_start, block * width_p, wide, 0)
    counted = lax.dynamic_slice_in_dim(padded_count, block, 2 * REACH + 1, 0)[column // width_p]
    inside = (block + offset_of >= 0) & (block + offset_of < nblk)
    tested = inside & (slot_of < counted) & (jnp.abs(offset_of) <= reach[0])
    tested = tested[None, :] & (jnp.abs(positions[:, None] - starts[None, :]) <= WIN)
    samples = rows * lax.axis_size("sample")
    scale = jnp.sqrt(jnp.float32(samples - ncov - 2))
    value = (
        scale * mine / (jnp.sqrt(gnorm_mine + 1e-06)[:, None] * jnp.sqrt(pnorm + 1e-06)[None, :])
    )
    return jnp.where(tested, value, jnp.float32(0.0))


F32 = jnp.float32
BF16 = jnp.bfloat16
MESH = pl.DeviceIdType.MESH
HIGH = lax.Precision.HIGHEST
PARTS = 8


def split3(value):
    hi = value.astype(BF16)
    rest = value - hi.astype(F32)
    mid = rest.astype(BF16)
    lo = (rest - mid.astype(F32)).astype(BF16)
    return hi, mid, lo


def scan_kernel(
    ncov, scale, geno_hbm, probe_hbm, cov_ref, out_ref,
    geno, probe, basis, base, stack, geno_t, around, sib_own, sib_next, acc, gathered,
    share, coef6, coefp, bgr, infos, pnorms, pnorms_in, acc_in,
    load_sem, x_send, x_recv, y_send, y_recv, c_send, c_recv, o_send, o_recv,
    g_send, g_recv, m_send, m_recv, n_send, n_recv, z_send, z_recv,
):
    rows, width_v = geno.shape
    width_p = probe.shape[1]
    part = rows // PARTS
    ncol = width_v + width_p
    g = lax.axis_index("genome")
    z = lax.axis_index("sample")
    core = g % 2
    x = (g // 2) % 2
    sib = g + 1 - 2 * core
    beside = g + 2 - 4 * x
    above = g + 4 - 8 * (g // 4)
    same = core * x + (1 - core) * (1 - x)
    onward = 1 - same

    def remote(src, dst, send, recv, **where):
        return pltpu.make_async_remote_copy(
            src_ref=src, dst_ref=dst, send_sem=send, recv_sem=recv,
            device_id=dict(where), device_id_type=MESH,
        )

    def sl(k):
        return pl.ds(pl.multiple_of(k * part, part), part)

    def x_copy(k):
        return remote(probe_hbm.at[sl(k)], around.at[0, sl(k)], x_send.at[k], x_recv.at[k], genome=beside)

    def y_copy(k):
        return remote(around.at[0, sl(k)], around.at[1, sl(k)], y_send.at[k], y_recv.at[k], genome=above)

    def c_copy(k):
        return remote(around.at[onward, sl(k)], sib_next.at[sl(k)], c_send.at[k], c_recv.at[k], genome=sib)

    own_copy = remote(probe_hbm, sib_own, o_send, o_recv, genome=sib)
    load_p = pltpu.make_async_copy(probe_hbm, probe, load_sem.at[0])
    load_g = pltpu.make_async_copy(geno_hbm, geno, load_sem.at[1])

    def peer(d):
        return (z + d) % 4

    def g_copy(d):
        return remote(share, gathered.at[d - 1], g_send.at[d - 1], g_recv.at[d - 1], sample=peer(d))

    def m_copy(n, d):
        return remote(infos.at[2], infos.at[2 - d], m_send.at[n], m_recv.at[n], genome=(g + d + 8) % 8)

    def n_copy(d):
        return remote(pnorms, pnorms_in.at[d - 1], n_send.at[d - 1], n_recv.at[d - 1], sample=peer(d))

    def z_copy(t, d):
        mine = pl.ds(pl.multiple_of(peer(d) * 128, 128), 128)
        return remote(acc.at[t, mine], acc_in.at[d - 1, t], z_send.at[t, d - 1], z_recv.at[t, d - 1], sample=peer(d))

    load_p.start()
    load_g.start()
    barrier = pltpu.get_barrier_semaphore()
    near = [sib, beside, above] + [(g + d + 8) % 8 for d in (1, 2, -1, -2)]
    for other in near:
        pl.semaphore_signal(barrier, inc=1, device_id={"genome": other}, device_id_type=MESH)
    for d in (1, 2, 3):
        pl.semaphore_signal(barrier, inc=1, device_id={"sample": peer(d)}, device_id_type=MESH)
    pl.semaphore_wait(barrier, len(near) + 3)

    @pl.loop(0, PARTS)
    def _(k):
        x_copy(k).start()

    own_copy.start()

    basis[...] = jnp.zeros_like(basis)
    base[...] = jnp.zeros_like(base)
    share[...] = jnp.zeros_like(share)
    acc[...] = jnp.zeros_like(acc)
    bgr[...] = jnp.zeros_like(bgr)
    load_p.wait()
    load_g.wait()

    @pl.loop(0, PARTS)
    def _(k):
        basis[0:ncov, :] = cov_ref[:, sl(k)]
        basis[ncov : ncov + 1, :] = jnp.ones((1, part), F32)
        b = basis[...]
        hi, mid, lo = split3(b)
        for n, piece in enumerate((hi, hi, mid, hi, mid, lo)):
            stack[k, 32 * n : 32 * n + 32, :] = piece
        b3 = stack[k, 96:192, :]
        both = ((geno, 0, width_v), (probe, width_v, width_p))
        for ref, first, width in both:
            got = jnp.dot(b3, ref[sl(k), :], preferred_element_type=F32)
            share[:, first : first + width] += got[0:32] + got[32:64] + got[64:96]
        base[0:32, :] = b
        share[:, ncol : ncol + 128] += lax.dot_general(
            b, base[...], (((1,), (1,)), ((), ())), precision=HIGH, preferred_element_type=F32
        )

    for d in (1, 2, 3):
        g_copy(d).start()
    x_copy(0).wait_recv()
    y_copy(0).start()
    for d in (1, 2, 3):
        g_copy(d).wait_recv()
    lane = lax.broadcasted_iota(jnp.int32, (32, 128), 1)
    line = lax.broadcasted_iota(jnp.int32, (32, ncol + 128), 0)

    def eliminate(k, a):
        col = jnp.sum(jnp.where(lane == k, a[:, ncol:], 0.0), axis=1, keepdims=True)
        row = jnp.sum(jnp.where(line == k, a, 0.0), axis=0, keepdims=True)
        pivot = jnp.sum(jnp.where(lane[0:1] == k, row[:, ncol:], 0.0), axis=1, keepdims=True)
        row = row / pivot
        return jnp.where(line == k, row, a - col * row)

    solved = lax.fori_loop(
        0, ncov + 1, eliminate, share[...] + gathered[0] + gathered[1] + gathered[2]
    )
    hi, mid, lo = split3(solved[:, 0:ncol])
    for n, piece in enumerate((hi, mid, hi, lo, mid, hi)):
        coef6[32 * n : 32 * n + 32, :] = piece
    infos[2] = solved[:, width_v:ncol]

    @pl.loop(0, PARTS)
    def _(k):
        fit = lax.dot_general(
            stack[k], coef6[:, width_v:ncol], (((0,), (0,)), ((), ())), preferred_element_type=F32
        )
        res = (probe[sl(k), :].astype(F32) - fit).astype(BF16).astype(F32)
        infos[2, 24:25, :] += jnp.sum(res * res, axis=0, keepdims=True)

    for n, d in enumerate((1, 2, -1, -2)):
        m_copy(n, d).start()
    x_copy(1).wait_recv()
    y_copy(1).start()

    def residual(k):
        fit = lax.dot_general(
            coef6[:, 0:width_v], stack[k], (((0,), (0,)), ((), ())), preferred_element_type=F32
        )
        res = (jnp.transpose(geno[sl(k), :]).astype(F32) - fit).astype(BF16)
        geno_t[k] = res
        bgr[...] += lax.dot_general(
            res, stack[k, 96:192, :], (((1,), (1,)), ((), ())), preferred_element_type=F32
        )
        acc[0] += jnp.dot(res, probe[sl(k), :], preferred_element_type=F32)
        wide = res.astype(F32)
        wide = wide * wide
        total = wide[:, 0:128]
        for n in range(1, part // 128):
            total = total + wide[:, 128 * n : 128 * n + 128]
        acc[5] += total

    @pl.loop(0, PARTS // 2)
    def _(i):
        residual(2 * i)
        residual(2 * i + 1)
        x_copy(i + 2).wait_recv()
        y_copy(i + 2).start()

    for n, d in enumerate((1, 2, -1, -2)):
        m_copy(n, d).wait_recv()
    for j in range(5):
        pnorms[j] = jnp.broadcast_to(infos[j, 24:25, :], (8, 128))
    for d in (1, 2, 3):
        n_copy(d).start()

    places = (2, 3 - 2 * core, 4 - 4 * x, 4 * x, 1 + 2 * core)

    def correct(t):
        for n in range(3):
            coefp[32 * n : 32 * n + 32, :] = infos[places[t]]
        acc[t] = acc[t] - jnp.dot(
            bgr[...], coefp[...], precision=HIGH, preferred_element_type=F32
        )

    own_copy.wait_recv()

    @pl.loop(0, PARTS)
    def _(k):
        acc[1] += jnp.dot(geno_t[k], sib_own[sl(k), :], preferred_element_type=F32)

    for t in range(5):
        correct(t)
    for t in (0, 1, 5):
        for d in (1, 2, 3):
            z_copy(t, d).start()

    def arrive(k):
        y_copy(k).wait_recv()
        c_copy(k).start()
        acc[2] += jnp.dot(geno_t[k], around[0, sl(k), :], preferred_element_type=F32)
        acc[3] += jnp.dot(geno_t[k], around[1, sl(k), :], preferred_element_type=F32)

    def beside_next(k):
        c_copy(k).wait_recv()
        acc[4] += jnp.dot(geno_t[k], sib_next[sl(k), :], preferred_element_type=F32)

    for k in (6, 7):
        arrive(k - 6)
        x_copy(k).wait_recv()
        y_copy(k).start()
    beside_next(0)

    @pl.loop(2, PARTS)
    def _(k):
        arrive(k)
        beside_next(k - 1)

    for t in (2, 3):
        for d in (1, 2, 3):
            z_copy(t, d).start()
    beside_next(PARTS - 1)
    for d in (1, 2, 3):
        z_copy(4, d).start()

    for d in (1, 2, 3):
        n_copy(d).wait_recv()
    mine = pl.ds(pl.multiple_of(z * 128, 128), 128)

    def total(t):
        for d in (1, 2, 3):
            z_copy(t, d).wait_recv()
        return acc[t, mine] + acc_in[0, t] + acc_in[1, t] + acc_in[2, t]

    gnorm = jnp.sqrt(jnp.sum(total(5), axis=1, keepdims=True) + 1e-06)
    for t in range(5):
        j = places[t]
        pn = pnorms[j] + pnorms_in[0, j] + pnorms_in[1, j] + pnorms_in[2, j]
        pn = jnp.sqrt(pn[0:1] + 1e-06)
        out_ref[:, pl.ds(pl.multiple_of(j * 128, 128), 128)] = scale * total(t) / (gnorm * pn)

    own_copy.wait_send()
    for n, d in enumerate((1, 2, -1, -2)):
        m_copy(n, d).wait_send()
    for d in (1, 2, 3):
        g_copy(d).wait_send()
        n_copy(d).wait_send()
        for t in range(6):
            z_copy(t, d).wait_send()

    @pl.loop(0, PARTS)
    def _(k):
        x_copy(k).wait_send()
        y_copy(k).wait_send()
        c_copy(k).wait_send()


def scan(genotypes, probes, covariates, total_rows):
    rows, width_v = genotypes.shape
    width_p = probes.shape[1]
    ncov = covariates.shape[0]
    part = rows // PARTS
    ncol = width_v + width_p
    dma = pltpu.SemaphoreType.DMA
    scale = float(total_rows - ncov - 2) ** 0.5
    block = jax.ShapeDtypeStruct((128, 5 * width_p), F32)

    scratch = [
        pltpu.VMEM((rows, width_v), BF16),
        pltpu.VMEM((rows, width_p), BF16),
        pltpu.VMEM((32, part), F32),
        pltpu.VMEM((128, part), F32),
        pltpu.VMEM((PARTS, 192, part), BF16),
        pltpu.VMEM((PARTS, width_v, part), BF16),
        pltpu.VMEM((2, rows, width_p), BF16),
        pltpu.VMEM((rows, width_p), BF16),
        pltpu.VMEM((rows, width_p), BF16),
        pltpu.VMEM((6, width_v, 128), F32),
        pltpu.VMEM((3, 32, ncol + 128), F32),
        pltpu.VMEM((32, ncol + 128), F32),
        pltpu.VMEM((192, ncol), BF16),
        pltpu.VMEM((96, 128), F32),
        pltpu.VMEM((width_v, 96), F32),
        pltpu.VMEM((5, 32, 128), F32),
        pltpu.VMEM((5, 8, 128), F32),
        pltpu.VMEM((3, 5, 8, 128), F32),
        pltpu.VMEM((3, 6, 128, 128), F32),
        dma((2,)),
        dma((PARTS,)), dma((PARTS,)), dma((PARTS,)), dma((PARTS,)), dma((PARTS,)), dma((PARTS,)),
        dma, dma,
        dma((3,)), dma((3,)), dma((4,)), dma((4,)), dma((3,)), dma((3,)), dma((6, 3)), dma((6, 3)),
    ]
    return pl.pallas_call(
        functools.partial(scan_kernel, ncov, scale),
        out_shape=block,
        in_specs=[
            pl.BlockSpec(memory_space=pl.ANY),
            pl.BlockSpec(memory_space=pl.ANY),
            pl.BlockSpec(memory_space=pltpu.VMEM),
        ],
        out_specs=pl.BlockSpec(memory_space=pltpu.VMEM),
        scratch_shapes=scratch,
        cost_estimate=pl.CostEstimate(flops=8 * 10**9, bytes_accessed=12 * 10**6, transcendentals=0),
        compiler_params=pltpu.CompilerParams(
            collective_id=0, has_side_effects=True, vmem_limit_bytes=56 * 2**20
        ),
    )(genotypes, probes, covariates)


def fused(genotypes, probes, covariates, probe_locus, probe_counts, reach, positions):
    width_p = probes.shape[1]
    nblk = probe_counts.shape[0]
    wide = (2 * REACH + 1) * width_p
    samples = genotypes.shape[0] * lax.axis_size("sample")
    value = scan(genotypes, probes, covariates, samples)
    block = lax.axis_index("genome")
    column = jnp.arange(wide, dtype=jnp.int32)
    offset_of = column // width_p - REACH
    slot_of = column % width_p
    padded_start = jnp.pad(probe_locus, (REACH * width_p, REACH * width_p))
    padded_count = jnp.pad(probe_counts, (REACH, REACH))
    starts = lax.dynamic_slice_in_dim(padded_start, block * width_p, wide, 0)
    counted = lax.dynamic_slice_in_dim(padded_count, block, 2 * REACH + 1, 0)[column // width_p]
    inside = (block + offset_of >= 0) & (block + offset_of < nblk)
    tested = inside & (slot_of < counted) & (jnp.abs(offset_of) <= reach[0])
    tested = tested[None, :] & (jnp.abs(positions[:, None] - starts[None, :]) <= WIN)
    return jnp.where(tested, value, jnp.float32(0.0))


def solution(mesh):
    placed = (
        P("sample", "genome"),
        P("sample", "genome"),
        P(None, "sample"),
        P(),
        P(),
        P("genome"),
        P(("genome", "sample")),
    )
    sizes = (mesh.shape["genome"], mesh.shape["sample"])
    return jax.shard_map(
        fused if sizes == (8, 4) else local, mesh=mesh, in_specs=placed, out_specs=P(("genome", "sample"), None), check_vma=False
    )
```

```python
import functools

import jax
import jax.numpy as jnp
from jax import lax
from jax.experimental import pallas as pl
from jax.experimental.pallas import tpu as pltpu
from jax.sharding import PartitionSpec as P

REACH = 2
WIN = 10000


def from_behind(value, axis, steps):
    count = lax.axis_size(axis)
    first, last = (max(0, -steps), min(count, count - steps))
    return lax.ppermute(value, axis, [(source, source + steps) for source in range(first, last)])


def fitted_part(data, basis, coef_sum, factor):
    coef = jax.scipy.linalg.cho_solve((factor, True), coef_sum)
    fitted = jnp.dot(basis.T, coef, precision=lax.Precision.HIGHEST)
    return (data.astype(jnp.float32) - fitted).astype(jnp.bfloat16)


def variant_products(left, right):
    return lax.dot_general(
        left, right, (((0,), (0,)), ((), ())), preferred_element_type=jnp.float32
    )


def local(genotypes, probes, covariates, probe_locus, probe_counts, reach, positions):
    rows = genotypes.shape[0]
    width_v = genotypes.shape[1]
    width_p = probes.shape[1]
    ncov = covariates.shape[0]
    nblk = probe_counts.shape[0]
    wide = (2 * REACH + 1) * width_p
    basis = jnp.concatenate([jnp.ones((1, rows), jnp.float32), covariates], 0)
    gram = jnp.dot(basis, basis.T, precision=lax.Precision.HIGHEST)
    cross_geno = jnp.dot(basis, genotypes.astype(jnp.float32), precision=lax.Precision.HIGHEST)
    cross_probe = jnp.dot(basis, probes.astype(jnp.float32), precision=lax.Precision.HIGHEST)
    gram, cross_geno, cross_probe = lax.psum((gram, cross_geno, cross_probe), "sample")
    factor = jnp.linalg.cholesky(gram)
    geno_res = fitted_part(genotypes, basis, cross_geno, factor)
    probe_res = fitted_part(probes, basis, cross_probe, factor)
    pieces = {0: probe_res}
    for direction in (1, -1):
        current = probe_res
        for stepper in range(1, REACH + 1):
            current = from_behind(current, "genome", -direction)
            pieces[direction * stepper] = current
    window = jnp.concatenate([pieces[offset] for offset in range(-REACH, REACH + 1)], 1)
    gres32 = geno_res.astype(jnp.float32)
    win32 = window.astype(jnp.float32)
    gnorm, pnorm = lax.psum((jnp.sum(gres32 * gres32, 0), jnp.sum(win32 * win32, 0)), "sample")
    share = width_v // lax.axis_size("sample")
    first_row = lax.axis_index("sample") * share
    total = lax.psum(variant_products(geno_res, window), "sample")
    mine = lax.dynamic_slice_in_dim(total, first_row, share, 0)
    gnorm_mine = lax.dynamic_slice_in_dim(gnorm, first_row, share, 0)
    block = lax.axis_index("genome")
    column = jnp.arange(wide, dtype=jnp.int32)
    offset_of = column // width_p - REACH
    slot_of = column % width_p
    padded_start = jnp.pad(probe_locus, (REACH * width_p, REACH * width_p))
    padded_count = jnp.pad(probe_counts, (REACH, REACH))
    starts = lax.dynamic_slice_in_dim(padded_start, block * width_p, wide, 0)
    counted = lax.dynamic_slice_in_dim(padded_count, block, 2 * REACH + 1, 0)[column // width_p]
    inside = (block + offset_of >= 0) & (block + offset_of < nblk)
    tested = inside & (slot_of < counted) & (jnp.abs(offset_of) <= reach[0])
    tested = tested[None, :] & (jnp.abs(positions[:, None] - starts[None, :]) <= WIN)
    samples = rows * lax.axis_size("sample")
    scale = jnp.sqrt(jnp.float32(samples - ncov - 2))
    value = (
        scale * mine / (jnp.sqrt(gnorm_mine + 1e-06)[:, None] * jnp.sqrt(pnorm + 1e-06)[None, :])
    )
    return jnp.where(tested, value, jnp.float32(0.0))


F32 = jnp.float32
BF16 = jnp.bfloat16
MESH = pl.DeviceIdType.MESH
HIGH = lax.Precision.HIGHEST
PARTS = 8


def split3(value):
    hi = value.astype(BF16)
    rest = value - hi.astype(F32)
    mid = rest.astype(BF16)
    lo = (rest - mid.astype(F32)).astype(BF16)
    return hi, mid, lo


def scan_kernel(
    ncov, scale, geno_hbm, probe_hbm, cov_ref, out_ref,
    geno, probe, basis, base, stack, geno_t, around, sib_own, sib_next, acc, gathered,
    share, coef6, coefp, bgr, infos, pnorms, pnorms_in, acc_in, late, late_in,
    load_sem, x_send, x_recv, y_send, y_recv, c_send, c_recv, o_send, o_recv,
    g_send, g_recv, m_send, m_recv, n_send, n_recv, z_send, z_recv,
):
    rows, width_v = geno.shape
    width_p = probe.shape[1]
    part = rows // PARTS
    ncol = width_v + width_p
    g = lax.axis_index("genome")
    z = lax.axis_index("sample")
    core = g % 2
    x = (g // 2) % 2
    sib = g + 1 - 2 * core
    beside = g + 2 - 4 * x
    above = g + 4 - 8 * (g // 4)
    same = core * x + (1 - core) * (1 - x)
    onward = 1 - same

    def remote(src, dst, send, recv, **where):
        return pltpu.make_async_remote_copy(
            src_ref=src, dst_ref=dst, send_sem=send, recv_sem=recv,
            device_id=dict(where), device_id_type=MESH,
        )

    def sl(k):
        return pl.ds(pl.multiple_of(k * part, part), part)

    def x_copy(k):
        return remote(probe_hbm.at[sl(k)], around.at[0, sl(k)], x_send.at[k], x_recv.at[k], genome=beside)

    def y_copy(k):
        return remote(around.at[0, sl(k)], around.at[1, sl(k)], y_send.at[k], y_recv.at[k], genome=above)

    def c_copy(k):
        return remote(around.at[onward, sl(k)], sib_next.at[sl(k)], c_send.at[k], c_recv.at[k], genome=sib)

    own_copy = remote(probe_hbm, sib_own, o_send, o_recv, genome=sib)
    load_p = pltpu.make_async_copy(probe_hbm, probe, load_sem.at[0])
    load_g = pltpu.make_async_copy(geno_hbm, geno, load_sem.at[1])

    def peer(d):
        return (z + d) % 4

    def g_copy(d):
        return remote(share, gathered.at[d - 1], g_send.at[d - 1], g_recv.at[d - 1], sample=peer(d))

    def m_copy(n, d):
        return remote(infos.at[2], infos.at[2 - d], m_send.at[n], m_recv.at[n], genome=(g + d + 8) % 8)

    def n_copy(d):
        return remote(pnorms, pnorms_in.at[d - 1], n_send.at[d - 1], n_recv.at[d - 1], sample=peer(d))

    def z_copy(t, d):
        mine = pl.ds(pl.multiple_of(peer(d) * 128, 128), 128)
        if 2 <= t <= 4:
            return remote(
                late.at[t - 2, mine], late_in.at[d - 1, t - 2],
                z_send.at[t, d - 1], z_recv.at[t, d - 1], sample=peer(d),
            )
        return remote(acc.at[t, mine], acc_in.at[d - 1, t], z_send.at[t, d - 1], z_recv.at[t, d - 1], sample=peer(d))

    load_p.start()
    load_g.start()
    barrier = pltpu.get_barrier_semaphore()
    near = [sib, beside, above] + [(g + d + 8) % 8 for d in (1, 2, -1, -2)]
    for other in near:
        pl.semaphore_signal(barrier, inc=1, device_id={"genome": other}, device_id_type=MESH)
    for d in (1, 2, 3):
        pl.semaphore_signal(barrier, inc=1, device_id={"sample": peer(d)}, device_id_type=MESH)
    pl.semaphore_wait(barrier, len(near) + 3)

    @pl.loop(0, PARTS)
    def _(k):
        x_copy(k).start()

    own_copy.start()

    def onto(k):
        x_copy(k).wait_recv()
        y_copy(k).start()

    basis[...] = jnp.zeros_like(basis)
    base[...] = jnp.zeros_like(base)
    share[...] = jnp.zeros_like(share)
    acc[...] = jnp.zeros_like(acc)
    bgr[...] = jnp.zeros_like(bgr)
    load_p.wait()
    load_g.wait()

    def crossed(k):
        basis[0:ncov, :] = cov_ref[:, sl(k)]
        basis[ncov : ncov + 1, :] = jnp.ones((1, part), F32)
        b = basis[...]
        hi, mid, lo = split3(b)
        for n, piece in enumerate((hi, hi, mid, hi, mid, lo)):
            stack[k, 32 * n : 32 * n + 32, :] = piece
        b3 = stack[k, 96:192, :]
        both = ((geno, 0, width_v), (probe, width_v, width_p))
        for ref, first, width in both:
            got = jnp.dot(b3, ref[sl(k), :], preferred_element_type=F32)
            share[:, first : first + width] += got[0:32] + got[32:64] + got[64:96]
        base[0:32, :] = b
        share[:, ncol : ncol + 128] += lax.dot_general(
            b, base[...], (((1,), (1,)), ((), ())), precision=HIGH, preferred_element_type=F32
        )

    pl.loop(0, PARTS - 2)(crossed)
    onto(0)
    pl.loop(PARTS - 2, PARTS)(crossed)
    for d in (1, 2, 3):
        g_copy(d).start()
    onto(1)
    for d in (1, 2, 3):
        g_copy(d).wait_recv()
    lane = lax.broadcasted_iota(jnp.int32, (32, 128), 1)
    line = lax.broadcasted_iota(jnp.int32, (32, ncol + 128), 0)

    def eliminate(k, a):
        col = jnp.sum(jnp.where(lane == k, a[:, ncol:], 0.0), axis=1, keepdims=True)
        row = jnp.sum(jnp.where(line == k, a, 0.0), axis=0, keepdims=True)
        pivot = jnp.sum(jnp.where(lane[0:1] == k, row[:, ncol:], 0.0), axis=1, keepdims=True)
        row = row / pivot
        return jnp.where(line == k, row, a - col * row)

    solved = share[...] + gathered[0] + gathered[1] + gathered[2]
    half = (ncov + 1) // 2
    solved = lax.fori_loop(0, half, eliminate, solved)
    onto(2)
    solved = lax.fori_loop(half, ncov + 1, eliminate, solved)
    onto(3)
    hi, mid, lo = split3(solved[:, 0:ncol])
    for n, piece in enumerate((hi, mid, hi, lo, mid, hi)):
        coef6[32 * n : 32 * n + 32, :] = piece
    infos[2] = solved[:, width_v:ncol]

    @pl.loop(0, PARTS)
    def _(k):
        fit = lax.dot_general(
            stack[k], coef6[:, width_v:ncol], (((0,), (0,)), ((), ())), preferred_element_type=F32
        )
        res = (probe[sl(k), :].astype(F32) - fit).astype(BF16).astype(F32)
        infos[2, 24:25, :] += jnp.sum(res * res, axis=0, keepdims=True)

    for n, d in enumerate((1, 2, -1, -2)):
        m_copy(n, d).start()
    onto(4)

    def residual(k):
        fit = lax.dot_general(
            coef6[:, 0:width_v], stack[k], (((0,), (0,)), ((), ())), preferred_element_type=F32
        )
        res = (jnp.transpose(geno[sl(k), :]).astype(F32) - fit).astype(BF16)
        geno_t[k] = res
        bgr[...] += lax.dot_general(
            res, stack[k, 96:192, :], (((1,), (1,)), ((), ())), preferred_element_type=F32
        )
        acc[0] += jnp.dot(res, probe[sl(k), :], preferred_element_type=F32)
        wide = res.astype(F32)
        wide = wide * wide
        total = wide[:, 0:128]
        for n in range(1, part // 128):
            total = total + wide[:, 128 * n : 128 * n + 128]
        acc[5] += total

    pl.loop(0, PARTS // 2)(residual)
    onto(5)
    pl.loop(PARTS // 2, PARTS)(residual)
    onto(6)

    for n, d in enumerate((1, 2, -1, -2)):
        m_copy(n, d).wait_recv()
    for j in range(5):
        pnorms[j] = jnp.broadcast_to(infos[j, 24:25, :], (8, 128))
    for d in (1, 2, 3):
        n_copy(d).start()

    places = (2, 3 - 2 * core, 4 - 4 * x, 4 * x, 1 + 2 * core)

    def correct(t):
        for n in range(3):
            coefp[32 * n : 32 * n + 32, :] = infos[places[t]]
        acc[t] = acc[t] - jnp.dot(
            bgr[...], coefp[...], precision=HIGH, preferred_element_type=F32
        )

    own_copy.wait_recv()

    @pl.loop(0, PARTS)
    def _(k):
        acc[1] += jnp.dot(geno_t[k], sib_own[sl(k), :], preferred_element_type=F32)

    for t in range(5):
        correct(t)
    for t in (0, 1, 5):
        for d in (1, 2, 3):
            z_copy(t, d).start()

    def arrive(k):
        y_copy(k).wait_recv()
        c_copy(k).start()
        acc[2] += jnp.dot(geno_t[k], around[0, sl(k), :], preferred_element_type=F32)
        acc[3] += jnp.dot(geno_t[k], around[1, sl(k), :], preferred_element_type=F32)

    def beside_next(k):
        c_copy(k).wait_recv()
        acc[4] += jnp.dot(geno_t[k], sib_next[sl(k), :], preferred_element_type=F32)

    arrive(0)
    onto(7)

    @pl.loop(1, PARTS)
    def _(k):
        arrive(k)
        beside_next(k - 1)

    for t in (2, 3):
        late[t - 2] = acc[t].astype(BF16)
        for d in (1, 2, 3):
            z_copy(t, d).start()
    beside_next(PARTS - 1)
    late[2] = acc[4].astype(BF16)
    for d in (1, 2, 3):
        z_copy(4, d).start()

    for d in (1, 2, 3):
        n_copy(d).wait_recv()
    mine = pl.ds(pl.multiple_of(z * 128, 128), 128)

    def total(t):
        for d in (1, 2, 3):
            z_copy(t, d).wait_recv()
        if 2 <= t <= 4:
            got = [late_in[n, t - 2].astype(F32) for n in range(3)]
            return acc[t, mine] + got[0] + got[1] + got[2]
        return acc[t, mine] + acc_in[0, t] + acc_in[1, t] + acc_in[2, t]

    gnorm = jnp.sqrt(jnp.sum(total(5), axis=1, keepdims=True) + 1e-06)
    for t in range(5):
        j = places[t]
        pn = pnorms[j] + pnorms_in[0, j] + pnorms_in[1, j] + pnorms_in[2, j]
        pn = jnp.sqrt(pn[0:1] + 1e-06)
        out_ref[:, pl.ds(pl.multiple_of(j * 128, 128), 128)] = scale * total(t) / (gnorm * pn)

    own_copy.wait_send()
    for n, d in enumerate((1, 2, -1, -2)):
        m_copy(n, d).wait_send()
    for d in (1, 2, 3):
        g_copy(d).wait_send()
        n_copy(d).wait_send()
        for t in range(6):
            z_copy(t, d).wait_send()

    @pl.loop(0, PARTS)
    def _(k):
        x_copy(k).wait_send()
        y_copy(k).wait_send()
        c_copy(k).wait_send()


def scan(genotypes, probes, covariates, total_rows):
    rows, width_v = genotypes.shape
    width_p = probes.shape[1]
    ncov = covariates.shape[0]
    part = rows // PARTS
    ncol = width_v + width_p
    dma = pltpu.SemaphoreType.DMA
    scale = float(total_rows - ncov - 2) ** 0.5
    block = jax.ShapeDtypeStruct((128, 5 * width_p), F32)

    scratch = [
        pltpu.VMEM((rows, width_v), BF16),
        pltpu.VMEM((rows, width_p), BF16),
        pltpu.VMEM((32, part), F32),
        pltpu.VMEM((128, part), F32),
        pltpu.VMEM((PARTS, 192, part), BF16),
        pltpu.VMEM((PARTS, width_v, part), BF16),
        pltpu.VMEM((2, rows, width_p), BF16),
        pltpu.VMEM((rows, width_p), BF16),
        pltpu.VMEM((rows, width_p), BF16),
        pltpu.VMEM((6, width_v, 128), F32),
        pltpu.VMEM((3, 32, ncol + 128), F32),
        pltpu.VMEM((32, ncol + 128), F32),
        pltpu.VMEM((192, ncol), BF16),
        pltpu.VMEM((96, 128), F32),
        pltpu.VMEM((width_v, 96), F32),
        pltpu.VMEM((5, 32, 128), F32),
        pltpu.VMEM((5, 8, 128), F32),
        pltpu.VMEM((3, 5, 8, 128), F32),
        pltpu.VMEM((3, 6, 128, 128), F32),
        pltpu.VMEM((3, width_v, 128), BF16),
        pltpu.VMEM((3, 3, 128, 128), BF16),
        dma((2,)),
        dma((PARTS,)), dma((PARTS,)), dma((PARTS,)), dma((PARTS,)), dma((PARTS,)), dma((PARTS,)),
        dma, dma,
        dma((3,)), dma((3,)), dma((4,)), dma((4,)), dma((3,)), dma((3,)), dma((6, 3)), dma((6, 3)),
    ]
    return pl.pallas_call(
        functools.partial(scan_kernel, ncov, scale),
        out_shape=block,
        in_specs=[
            pl.BlockSpec(memory_space=pl.ANY),
            pl.BlockSpec(memory_space=pl.ANY),
            pl.BlockSpec(memory_space=pltpu.VMEM),
        ],
        out_specs=pl.BlockSpec(memory_space=pltpu.VMEM),
        scratch_shapes=scratch,
        cost_estimate=pl.CostEstimate(flops=8 * 10**9, bytes_accessed=12 * 10**6, transcendentals=0),
        compiler_params=pltpu.CompilerParams(
            collective_id=0, has_side_effects=True, vmem_limit_bytes=56 * 2**20
        ),
    )(genotypes, probes, covariates)


def fused(genotypes, probes, covariates, probe_locus, probe_counts, reach, positions):
    width_p = probes.shape[1]
    nblk = probe_counts.shape[0]
    wide = (2 * REACH + 1) * width_p
    samples = genotypes.shape[0] * lax.axis_size("sample")
    value = scan(genotypes, probes, covariates, samples)
    block = lax.axis_index("genome")
    offset = jnp.arange(-REACH, REACH + 1, dtype=jnp.int32)[:, None]
    slot = jnp.arange(width_p, dtype=jnp.int32)[None, :]
    padded_start = jnp.pad(probe_locus, (REACH * width_p, REACH * width_p))
    padded_count = jnp.pad(probe_counts, (REACH, REACH))
    starts = lax.dynamic_slice_in_dim(padded_start, block * width_p, wide, 0)
    counted = lax.dynamic_slice_in_dim(padded_count, block, 2 * REACH + 1, 0)[:, None]
    inside = (block + offset >= 0) & (block + offset < nblk)
    valid = inside & (slot < counted) & (jnp.abs(offset) <= reach[0])
    limit = jnp.where(valid, WIN, -1).reshape(wide)
    tested = jnp.abs(positions[:, None] - starts[None, :]) <= limit[None, :]
    return jnp.where(tested, value, jnp.float32(0.0))


def solution(mesh):
    placed = (
        P("sample", "genome"),
        P("sample", "genome"),
        P(None, "sample"),
        P(),
        P(),
        P("genome"),
        P(("genome", "sample")),
    )
    sizes = (mesh.shape["genome"], mesh.shape["sample"])
    return jax.shard_map(
        fused if sizes == (8, 4) else local, mesh=mesh, in_specs=placed, out_specs=P(("genome", "sample"), None), check_vma=False
    )
```

```python
import functools

import jax
import jax.numpy as jnp
from jax import lax
from jax.experimental import pallas as pl
from jax.experimental.pallas import tpu as pltpu
from jax.sharding import PartitionSpec as P

REACH = 2
WIN = 10000


def from_behind(value, axis, steps):
    count = lax.axis_size(axis)
    first, last = (max(0, -steps), min(count, count - steps))
    return lax.ppermute(value, axis, [(source, source + steps) for source in range(first, last)])


def fitted_part(data, basis, coef_sum, factor):
    coef = jax.scipy.linalg.cho_solve((factor, True), coef_sum)
    fitted = jnp.dot(basis.T, coef, precision=lax.Precision.HIGHEST)
    return (data.astype(jnp.float32) - fitted).astype(jnp.bfloat16)


def variant_products(left, right):
    return lax.dot_general(
        left, right, (((0,), (0,)), ((), ())), preferred_element_type=jnp.float32
    )


def local(genotypes, probes, covariates, probe_locus, probe_counts, reach, positions):
    rows = genotypes.shape[0]
    width_v = genotypes.shape[1]
    width_p = probes.shape[1]
    ncov = covariates.shape[0]
    nblk = probe_counts.shape[0]
    wide = (2 * REACH + 1) * width_p
    basis = jnp.concatenate([jnp.ones((1, rows), jnp.float32), covariates], 0)
    gram = jnp.dot(basis, basis.T, precision=lax.Precision.HIGHEST)
    cross_geno = jnp.dot(basis, genotypes.astype(jnp.float32), precision=lax.Precision.HIGHEST)
    cross_probe = jnp.dot(basis, probes.astype(jnp.float32), precision=lax.Precision.HIGHEST)
    gram, cross_geno, cross_probe = lax.psum((gram, cross_geno, cross_probe), "sample")
    factor = jnp.linalg.cholesky(gram)
    geno_res = fitted_part(genotypes, basis, cross_geno, factor)
    probe_res = fitted_part(probes, basis, cross_probe, factor)
    pieces = {0: probe_res}
    for direction in (1, -1):
        current = probe_res
        for stepper in range(1, REACH + 1):
            current = from_behind(current, "genome", -direction)
            pieces[direction * stepper] = current
    window = jnp.concatenate([pieces[offset] for offset in range(-REACH, REACH + 1)], 1)
    gres32 = geno_res.astype(jnp.float32)
    win32 = window.astype(jnp.float32)
    gnorm, pnorm = lax.psum((jnp.sum(gres32 * gres32, 0), jnp.sum(win32 * win32, 0)), "sample")
    share = width_v // lax.axis_size("sample")
    first_row = lax.axis_index("sample") * share
    total = lax.psum(variant_products(geno_res, window), "sample")
    mine = lax.dynamic_slice_in_dim(total, first_row, share, 0)
    gnorm_mine = lax.dynamic_slice_in_dim(gnorm, first_row, share, 0)
    block = lax.axis_index("genome")
    column = jnp.arange(wide, dtype=jnp.int32)
    offset_of = column // width_p - REACH
    slot_of = column % width_p
    padded_start = jnp.pad(probe_locus, (REACH * width_p, REACH * width_p))
    padded_count = jnp.pad(probe_counts, (REACH, REACH))
    starts = lax.dynamic_slice_in_dim(padded_start, block * width_p, wide, 0)
    counted = lax.dynamic_slice_in_dim(padded_count, block, 2 * REACH + 1, 0)[column // width_p]
    inside = (block + offset_of >= 0) & (block + offset_of < nblk)
    tested = inside & (slot_of < counted) & (jnp.abs(offset_of) <= reach[0])
    tested = tested[None, :] & (jnp.abs(positions[:, None] - starts[None, :]) <= WIN)
    samples = rows * lax.axis_size("sample")
    scale = jnp.sqrt(jnp.float32(samples - ncov - 2))
    value = (
        scale * mine / (jnp.sqrt(gnorm_mine + 1e-06)[:, None] * jnp.sqrt(pnorm + 1e-06)[None, :])
    )
    return jnp.where(tested, value, jnp.float32(0.0))


F32 = jnp.float32
BF16 = jnp.bfloat16
MESH = pl.DeviceIdType.MESH
HIGH = lax.Precision.HIGHEST
PARTS = 8


def split3(value):
    hi = value.astype(BF16)
    rest = value - hi.astype(F32)
    mid = rest.astype(BF16)
    lo = (rest - mid.astype(F32)).astype(BF16)
    return hi, mid, lo


def scan_kernel(
    ncov, scale, geno_hbm, probe_hbm, cov_ref, out_ref,
    geno, probe, basis, base, stack, geno_t, around, sib_own, sib_next, acc, gathered,
    share, coef6, coefp, bgr, infos, pnorms, pnorms_in, acc_in, late, late_in,
    load_sem, x_send, x_recv, y_send, y_recv, c_send, c_recv, o_send, o_recv,
    g_send, g_recv, m_send, m_recv, n_send, n_recv, z_send, z_recv,
):
    rows, width_v = geno.shape
    width_p = probe.shape[1]
    part = rows // PARTS
    ncol = width_v + width_p
    g = lax.axis_index("genome")
    z = lax.axis_index("sample")
    core = g % 2
    x = (g // 2) % 2
    sib = g + 1 - 2 * core
    beside = g + 2 - 4 * x
    above = g + 4 - 8 * (g // 4)
    same = core * x + (1 - core) * (1 - x)
    onward = 1 - same

    def remote(src, dst, send, recv, **where):
        return pltpu.make_async_remote_copy(
            src_ref=src, dst_ref=dst, send_sem=send, recv_sem=recv,
            device_id=dict(where), device_id_type=MESH,
        )

    def sl(k):
        return pl.ds(pl.multiple_of(k * part, part), part)

    def x_copy(k):
        return remote(probe_hbm.at[sl(k)], around.at[0, sl(k)], x_send.at[k], x_recv.at[k], genome=beside)

    def y_copy(k):
        return remote(around.at[0, sl(k)], around.at[1, sl(k)], y_send.at[k], y_recv.at[k], genome=above)

    def c_copy(k):
        return remote(around.at[onward, sl(k)], sib_next.at[sl(k)], c_send.at[k], c_recv.at[k], genome=sib)

    own_copy = remote(probe_hbm, sib_own, o_send, o_recv, genome=sib)
    load_p = pltpu.make_async_copy(probe_hbm, probe, load_sem.at[0])
    load_g = pltpu.make_async_copy(geno_hbm, geno, load_sem.at[1])

    def peer(d):
        return (z + d) % 4

    def g_copy(d):
        return remote(share, gathered.at[d - 1], g_send.at[d - 1], g_recv.at[d - 1], sample=peer(d))

    def m_copy(n, d):
        return remote(infos.at[2], infos.at[2 - d], m_send.at[n], m_recv.at[n], genome=(g + d + 8) % 8)

    def n_copy(d):
        return remote(pnorms, pnorms_in.at[d - 1], n_send.at[d - 1], n_recv.at[d - 1], sample=peer(d))

    def z_copy(t, d):
        mine = pl.ds(pl.multiple_of(peer(d) * 128, 128), 128)
        if 2 <= t <= 4:
            return remote(
                late.at[t - 2, mine], late_in.at[d - 1, t - 2],
                z_send.at[t, d - 1], z_recv.at[t, d - 1], sample=peer(d),
            )
        return remote(acc.at[t, mine], acc_in.at[d - 1, t], z_send.at[t, d - 1], z_recv.at[t, d - 1], sample=peer(d))

    load_p.start()
    load_g.start()
    barrier = pltpu.get_barrier_semaphore()
    near = [sib, beside, above] + [(g + d + 8) % 8 for d in (1, 2, -1, -2)]
    for other in near:
        pl.semaphore_signal(barrier, inc=1, device_id={"genome": other}, device_id_type=MESH)
    for d in (1, 2, 3):
        pl.semaphore_signal(barrier, inc=1, device_id={"sample": peer(d)}, device_id_type=MESH)
    pl.semaphore_wait(barrier, len(near) + 3)

    ahead = 3

    @pl.loop(0, ahead)
    def _(k):
        x_copy(k).start()

    own_copy.start()

    def onto(k):
        x_copy(k).wait_recv()
        y_copy(k).start()
        if k + ahead < PARTS:
            x_copy(k + ahead).start()

    basis[...] = jnp.zeros_like(basis)
    base[...] = jnp.zeros_like(base)
    share[...] = jnp.zeros_like(share)
    acc[...] = jnp.zeros_like(acc)
    bgr[...] = jnp.zeros_like(bgr)
    load_p.wait()
    load_g.wait()

    def crossed(k):
        basis[0:ncov, :] = cov_ref[:, sl(k)]
        basis[ncov : ncov + 1, :] = jnp.ones((1, part), F32)
        b = basis[...]
        hi, mid, lo = split3(b)
        for n, piece in enumerate((hi, hi, mid, hi, mid, lo)):
            stack[k, 32 * n : 32 * n + 32, :] = piece
        b3 = stack[k, 96:192, :]
        both = ((geno, 0, width_v), (probe, width_v, width_p))
        for ref, first, width in both:
            got = jnp.dot(b3, ref[sl(k), :], preferred_element_type=F32)
            share[:, first : first + width] += got[0:32] + got[32:64] + got[64:96]
        base[0:32, :] = b
        share[:, ncol : ncol + 128] += lax.dot_general(
            b, base[...], (((1,), (1,)), ((), ())), precision=HIGH, preferred_element_type=F32
        )

    pl.loop(0, PARTS - 2)(crossed)
    onto(0)
    pl.loop(PARTS - 2, PARTS)(crossed)
    for d in (1, 2, 3):
        g_copy(d).start()
    onto(1)
    for d in (1, 2, 3):
        g_copy(d).wait_recv()
    lane = lax.broadcasted_iota(jnp.int32, (32, 128), 1)
    line = lax.broadcasted_iota(jnp.int32, (32, ncol + 128), 0)

    def eliminate(k, a):
        col = jnp.sum(jnp.where(lane == k, a[:, ncol:], 0.0), axis=1, keepdims=True)
        row = jnp.sum(jnp.where(line == k, a, 0.0), axis=0, keepdims=True)
        pivot = jnp.sum(jnp.where(lane[0:1] == k, row[:, ncol:], 0.0), axis=1, keepdims=True)
        row = row / pivot
        return jnp.where(line == k, row, a - col * row)

    solved = share[...] + gathered[0] + gathered[1] + gathered[2]
    half = (ncov + 1) // 2
    solved = lax.fori_loop(0, half, eliminate, solved)
    onto(2)
    solved = lax.fori_loop(half, ncov + 1, eliminate, solved)
    onto(3)
    hi, mid, lo = split3(solved[:, 0:ncol])
    for n, piece in enumerate((hi, mid, hi, lo, mid, hi)):
        coef6[32 * n : 32 * n + 32, :] = piece
    infos[2] = solved[:, width_v:ncol]

    @pl.loop(0, PARTS)
    def _(k):
        fit = lax.dot_general(
            stack[k], coef6[:, width_v:ncol], (((0,), (0,)), ((), ())), preferred_element_type=F32
        )
        res = (probe[sl(k), :].astype(F32) - fit).astype(BF16).astype(F32)
        infos[2, 24:25, :] += jnp.sum(res * res, axis=0, keepdims=True)

    for n, d in enumerate((1, 2, -1, -2)):
        m_copy(n, d).start()
    onto(4)

    def residual(k):
        fit = lax.dot_general(
            coef6[:, 0:width_v], stack[k], (((0,), (0,)), ((), ())), preferred_element_type=F32
        )
        res = (jnp.transpose(geno[sl(k), :]).astype(F32) - fit).astype(BF16)
        geno_t[k] = res
        bgr[...] += lax.dot_general(
            res, stack[k, 96:192, :], (((1,), (1,)), ((), ())), preferred_element_type=F32
        )
        acc[0] += jnp.dot(res, probe[sl(k), :], preferred_element_type=F32)
        wide = res.astype(F32)
        wide = wide * wide
        total = wide[:, 0:128]
        for n in range(1, part // 128):
            total = total + wide[:, 128 * n : 128 * n + 128]
        acc[5] += total

    pl.loop(0, PARTS // 2)(residual)
    onto(5)
    pl.loop(PARTS // 2, PARTS)(residual)
    onto(6)

    for n, d in enumerate((1, 2, -1, -2)):
        m_copy(n, d).wait_recv()
    for j in range(5):
        pnorms[j] = jnp.broadcast_to(infos[j, 24:25, :], (8, 128))
    for d in (1, 2, 3):
        n_copy(d).start()

    places = (2, 3 - 2 * core, 4 - 4 * x, 4 * x, 1 + 2 * core)

    def correct(t):
        for n in range(3):
            coefp[32 * n : 32 * n + 32, :] = infos[places[t]]
        acc[t] = acc[t] - jnp.dot(
            bgr[...], coefp[...], precision=HIGH, preferred_element_type=F32
        )

    own_copy.wait_recv()

    @pl.loop(0, PARTS)
    def _(k):
        acc[1] += jnp.dot(geno_t[k], sib_own[sl(k), :], preferred_element_type=F32)

    for t in range(5):
        correct(t)
    for t in (0, 1, 5):
        for d in (1, 2, 3):
            z_copy(t, d).start()

    def arrive(k):
        y_copy(k).wait_recv()
        c_copy(k).start()
        acc[2] += jnp.dot(geno_t[k], around[0, sl(k), :], preferred_element_type=F32)
        acc[3] += jnp.dot(geno_t[k], around[1, sl(k), :], preferred_element_type=F32)

    def beside_next(k):
        c_copy(k).wait_recv()
        acc[4] += jnp.dot(geno_t[k], sib_next[sl(k), :], preferred_element_type=F32)

    arrive(0)
    onto(7)

    @pl.loop(1, PARTS)
    def _(k):
        arrive(k)
        beside_next(k - 1)

    for t in (2, 3):
        late[t - 2] = acc[t].astype(BF16)
        for d in (1, 2, 3):
            z_copy(t, d).start()
    beside_next(PARTS - 1)
    late[2] = acc[4].astype(BF16)
    for d in (1, 2, 3):
        z_copy(4, d).start()

    for d in (1, 2, 3):
        n_copy(d).wait_recv()
    mine = pl.ds(pl.multiple_of(z * 128, 128), 128)

    def total(t):
        for d in (1, 2, 3):
            z_copy(t, d).wait_recv()
        if 2 <= t <= 4:
            got = [late_in[n, t - 2].astype(F32) for n in range(3)]
            return acc[t, mine] + got[0] + got[1] + got[2]
        return acc[t, mine] + acc_in[0, t] + acc_in[1, t] + acc_in[2, t]

    gnorm = jnp.sqrt(jnp.sum(total(5), axis=1, keepdims=True) + 1e-06)
    for t in range(5):
        j = places[t]
        pn = pnorms[j] + pnorms_in[0, j] + pnorms_in[1, j] + pnorms_in[2, j]
        pn = jnp.sqrt(pn[0:1] + 1e-06)
        out_ref[:, pl.ds(pl.multiple_of(j * 128, 128), 128)] = scale * total(t) / (gnorm * pn)

    own_copy.wait_send()
    for n, d in enumerate((1, 2, -1, -2)):
        m_copy(n, d).wait_send()
    for d in (1, 2, 3):
        g_copy(d).wait_send()
        n_copy(d).wait_send()
        for t in range(6):
            z_copy(t, d).wait_send()

    @pl.loop(0, PARTS)
    def _(k):
        x_copy(k).wait_send()
        y_copy(k).wait_send()
        c_copy(k).wait_send()


def scan(genotypes, probes, covariates, total_rows):
    rows, width_v = genotypes.shape
    width_p = probes.shape[1]
    ncov = covariates.shape[0]
    part = rows // PARTS
    ncol = width_v + width_p
    dma = pltpu.SemaphoreType.DMA
    scale = float(total_rows - ncov - 2) ** 0.5
    block = jax.ShapeDtypeStruct((128, 5 * width_p), F32)

    scratch = [
        pltpu.VMEM((rows, width_v), BF16),
        pltpu.VMEM((rows, width_p), BF16),
        pltpu.VMEM((32, part), F32),
        pltpu.VMEM((128, part), F32),
        pltpu.VMEM((PARTS, 192, part), BF16),
        pltpu.VMEM((PARTS, width_v, part), BF16),
        pltpu.VMEM((2, rows, width_p), BF16),
        pltpu.VMEM((rows, width_p), BF16),
        pltpu.VMEM((rows, width_p), BF16),
        pltpu.VMEM((6, width_v, 128), F32),
        pltpu.VMEM((3, 32, ncol + 128), F32),
        pltpu.VMEM((32, ncol + 128), F32),
        pltpu.VMEM((192, ncol), BF16),
        pltpu.VMEM((96, 128), F32),
        pltpu.VMEM((width_v, 96), F32),
        pltpu.VMEM((5, 32, 128), F32),
        pltpu.VMEM((5, 8, 128), F32),
        pltpu.VMEM((3, 5, 8, 128), F32),
        pltpu.VMEM((3, 6, 128, 128), F32),
        pltpu.VMEM((3, width_v, 128), BF16),
        pltpu.VMEM((3, 3, 128, 128), BF16),
        dma((2,)),
        dma((PARTS,)), dma((PARTS,)), dma((PARTS,)), dma((PARTS,)), dma((PARTS,)), dma((PARTS,)),
        dma, dma,
        dma((3,)), dma((3,)), dma((4,)), dma((4,)), dma((3,)), dma((3,)), dma((6, 3)), dma((6, 3)),
    ]
    return pl.pallas_call(
        functools.partial(scan_kernel, ncov, scale),
        out_shape=block,
        in_specs=[
            pl.BlockSpec(memory_space=pl.ANY),
            pl.BlockSpec(memory_space=pl.ANY),
            pl.BlockSpec(memory_space=pltpu.VMEM),
        ],
        out_specs=pl.BlockSpec(memory_space=pltpu.VMEM),
        scratch_shapes=scratch,
        cost_estimate=pl.CostEstimate(flops=8 * 10**9, bytes_accessed=12 * 10**6, transcendentals=0),
        compiler_params=pltpu.CompilerParams(
            collective_id=0, has_side_effects=True, vmem_limit_bytes=56 * 2**20
        ),
    )(genotypes, probes, covariates)


def fused(genotypes, probes, covariates, probe_locus, probe_counts, reach, positions):
    width_p = probes.shape[1]
    nblk = probe_counts.shape[0]
    wide = (2 * REACH + 1) * width_p
    samples = genotypes.shape[0] * lax.axis_size("sample")
    value = scan(genotypes, probes, covariates, samples)
    block = lax.axis_index("genome")
    offset = jnp.arange(-REACH, REACH + 1, dtype=jnp.int32)[:, None]
    slot = jnp.arange(width_p, dtype=jnp.int32)[None, :]
    padded_start = jnp.pad(probe_locus, (REACH * width_p, REACH * width_p))
    padded_count = jnp.pad(probe_counts, (REACH, REACH))
    starts = lax.dynamic_slice_in_dim(padded_start, block * width_p, wide, 0)
    counted = lax.dynamic_slice_in_dim(padded_count, block, 2 * REACH + 1, 0)[:, None]
    inside = (block + offset >= 0) & (block + offset < nblk)
    valid = inside & (slot < counted) & (jnp.abs(offset) <= reach[0])
    limit = jnp.where(valid, WIN, -1).reshape(wide)
    tested = jnp.abs(positions[:, None] - starts[None, :]) <= limit[None, :]
    return jnp.where(tested, value, jnp.float32(0.0))


def solution(mesh):
    placed = (
        P("sample", "genome"),
        P("sample", "genome"),
        P(None, "sample"),
        P(),
        P(),
        P("genome"),
        P(("genome", "sample")),
    )
    sizes = (mesh.shape["genome"], mesh.shape["sample"])
    return jax.shard_map(
        fused if sizes == (8, 4) else local, mesh=mesh, in_specs=placed, out_specs=P(("genome", "sample"), None), check_vma=False
    )
```
